512 devices in a mesh: prompt: 32 (over z, core), sample: 4 (over y), tensor: 4 (over x).
Axes of the slice: x: 4, y: 4, z: 16, core: 2. Of those that a mesh axis runs over, the one named last changes fastest.
Arguments:
- queries: bfloat16 [3, 160, 64, 128], P(None, 'sample', 'tensor'), may hold values from -12 to 65, as said below
- prefix_keys: bfloat16 [10, 16384, 8, 128], P(None, ('prompt', 'sample'), 'tensor'), may hold values from -9 to 40, as said below
- prefix_values: bfloat16 [10, 16384, 8, 128], P(None, ('prompt', 'sample'), 'tensor'), may hold values from -192 to 192
- suffix_keys: bfloat16 [160, 8, 8, 128], P('sample', None, 'tensor'), may hold values from -20 to 20
- suffix_values: bfloat16 [160, 8, 8, 128], P('sample', None, 'tensor'), may hold values from -192 to 192
- new_keys: bfloat16 [3, 160, 8, 128], P(None, 'sample', 'tensor'), may hold values from -20 to 20
- new_values: bfloat16 [3, 160, 8, 128], P(None, 'sample', 'tensor'), may hold values from -192 to 192
- prompt_lengths: int32 [10], replicated, may hold values from 5461 to 16384, as said below
- unfinished: int32 [3, 10], replicated, may hold values from 1 to 16, as said below
- slot_sample: int32 [160], replicated, may hold values from 0 to 159, each once
Outputs:
- attended: bfloat16 [3, 160, 64, 128], P(None, 'sample', 'tensor')
The draws below stay inside these ranges and needn't reach their ends.
Inputs may be any that keep to these rules, and one draw needn't show every extreme that they name: `queries`: query vectors of the new tokens. `prefix_keys`: key vectors of the prompts' prefixes. `prompt_lengths`: prefix positions at or beyond a prompt's length are not keys. Some prompt has exactly 16384 positions and some exactly 5461. The samples of prompt p with index below unfinished[t, p] are still generating at step t. `slot_sample`: each sample of each prompt is held by exactly one slot.
All inputs are finite; a program needn't handle non-finite values.
Results may differ from the reference program's by a relative error of at most 0.003.
Values may be sent and summed in bfloat16 or wider, within the bound.
No kernel may reach another device: no remote copies, remote signals or barrier semaphores. Data moves between devices by JAX's collectives and lax.ppermute only.
A program may use at most 64 MiB of HBM per device.

```python
import math
import jax
import jax.numpy as jnp
from jax import lax

HQ = 64
KVH = 8
HD = 128
SAMPLES = 16
STEPS = 3
PROMPTS = 10
SUF = 8
SLOTS = 160
LMAX = 16384


def draw_queries(key, part):
    key = jax.random.fold_in(key, 11)
    values = jnp.clip(jax.random.normal(key, (STEPS, SLOTS, HQ, HD), jnp.float32), -6.0, 6.0)
    return values.astype(jnp.bfloat16)


def draw_prefix_keys(key, part):
    key = jax.random.fold_in(key, 23)
    values = 1.5 * jnp.clip(jax.random.normal(key, (PROMPTS, LMAX, KVH, HD), jnp.float32), -6.0, 6.0)
    return values.astype(jnp.bfloat16)


def draw_prompt_lengths(key, part):
    key = jax.random.fold_in(key, 31)
    key_len, key_long = jax.random.split(key)
    lengths = jax.random.randint(key_len, (PROMPTS,), LMAX // 3, LMAX + 1)
    longest = jax.random.randint(key_long, (), 0, PROMPTS)
    indices = jnp.arange(PROMPTS, dtype=jnp.int32)
    lengths = jnp.where(indices == longest, LMAX, lengths)
    lengths = jnp.where(indices == (longest + 1) % PROMPTS, LMAX // 3, lengths)
    return lengths.astype(jnp.int32)


def draw_unfinished(key, part):
    key = jax.random.fold_in(key, 43)
    key_fresh, key_last = jax.random.split(key)
    fresh = jax.random.randint(key_fresh, (STEPS, PROMPTS), SAMPLES // 2, SAMPLES + 1)
    fresh = fresh.at[0].set(SAMPLES)
    running = jax.lax.cummin(fresh, axis=0)
    last = jax.random.randint(key_last, (), 0, PROMPTS)
    final = jnp.where(jnp.arange(PROMPTS, dtype=jnp.int32) == last, 1, running[STEPS - 1])
    running = running.at[STEPS - 1].set(final)
    return running.astype(jnp.int32)


def levels(own_key, shape, cuts, low, largest):
    loudness, own = 1.0, jax.random.fold_in(own_key, 6)
    for axis_at, parts in cuts:
        steps = jnp.exp(jax.random.uniform(jax.random.fold_in(own, axis_at), (parts,), jnp.float32, low / len(cuts), largest / len(cuts)))
        loudness = loudness * jnp.repeat(steps, shape[axis_at] // parts).reshape([-1 if axis == axis_at else 1 for axis in range(len(shape))])
    return loudness


def bell_draw(rng, dims, width, bound, cuts=(), kind=jnp.bfloat16):
    drawn = width * jax.random.normal(rng, dims, jnp.float32)
    if cuts:
        drawn = drawn * levels(rng, dims, cuts, -0.22, 0.18)
    return jnp.clip(drawn, -bound, bound).astype(kind)


def setup_inputs(seed: int = 0) -> dict:
    key_list = jax.random.split(jax.random.key(seed), 11)
    queries = draw_queries(jax.random.fold_in(key_list[10], 71), 0)
    prefix_keys = draw_prefix_keys(jax.random.fold_in(key_list[10], 71), 0)
    prefix_values = bell_draw(key_list[2], (PROMPTS, LMAX, KVH, HD), 32.0, 192.0, ((1, 128), (2, 4)))
    suffix_keys = bell_draw(key_list[3], (SLOTS, SUF, KVH, HD), 3.5, 20.0, ((0, 4), (2, 4)))
    suffix_values = bell_draw(key_list[4], (SLOTS, SUF, KVH, HD), 32.0, 192.0, ((0, 4), (2, 4)))
    new_keys = bell_draw(key_list[5], (STEPS, SLOTS, KVH, HD), 3.5, 20.0, ((1, 4), (2, 4)))
    new_values = bell_draw(key_list[6], (STEPS, SLOTS, KVH, HD), 32.0, 192.0, ((1, 4), (2, 4)))
    prompt_lengths = draw_prompt_lengths(jax.random.fold_in(key_list[10], 71), 0)
    unfinished = draw_unfinished(jax.random.fold_in(key_list[10], 71), 0)
    slot_sample = jax.random.permutation(key_list[9], SLOTS).astype(jnp.int32)
    return dict(queries=queries, prefix_keys=prefix_keys, prefix_values=prefix_values, suffix_keys=suffix_keys, suffix_values=suffix_values, new_keys=new_keys, new_values=new_values, prompt_lengths=prompt_lengths, unfinished=unfinished, slot_sample=slot_sample)


MASKED = -1e+30

def by_sample(array, sample_slot, axis):
    taken = jnp.take(array, sample_slot, axis=axis)
    shape = array.shape[:axis] + (PROMPTS, SAMPLES) + array.shape[axis + 1:]
    return taken.reshape(shape)

def rounded(weights):
    return lax.optimization_barrier(weights.astype(jnp.bfloat16)).astype(jnp.float32)

def reference(queries, prefix_keys, prefix_values, suffix_keys, suffix_values, new_keys, new_values, prompt_lengths, unfinished, slot_sample):
    group_size = HQ // KVH
    score_scale = 1.0 / math.sqrt(HD)
    sample_slot = jnp.argsort(slot_sample).astype(jnp.int32)
    query_sorted = by_sample(queries.astype(jnp.float32), sample_slot, 1)
    query_sorted = query_sorted.reshape(STEPS, PROMPTS, SAMPLES, KVH, group_size, HD)
    query_sorted = jnp.transpose(query_sorted, (1, 3, 0, 2, 4, 5))
    suffix_key_sorted = jnp.transpose(by_sample(suffix_keys.astype(jnp.float32), sample_slot, 0), (0, 3, 1, 2, 4))
    suffix_value_sorted = jnp.transpose(by_sample(suffix_values.astype(jnp.float32), sample_slot, 0), (0, 3, 1, 2, 4))
    new_key_sorted = jnp.transpose(by_sample(new_keys.astype(jnp.float32), sample_slot, 1), (1, 3, 0, 2, 4))
    new_value_sorted = jnp.transpose(by_sample(new_values.astype(jnp.float32), sample_slot, 1), (1, 3, 0, 2, 4))
    prefix_key_heads = jnp.transpose(prefix_keys.astype(jnp.float32), (0, 2, 1, 3))
    prefix_value_heads = jnp.transpose(prefix_values.astype(jnp.float32), (0, 2, 1, 3))
    positions = jnp.arange(LMAX, dtype=jnp.int32)
    step_ids = jnp.arange(STEPS, dtype=jnp.int32)
    causal = (step_ids[None, :] <= step_ids[:, None])[:, None, None, :]

    def one_prompt(inputs):
        query_block, key_block, value_block, suffix_key, suffix_value, new_key, new_value, length = inputs
        visible = positions < length

        def one_head(head_inputs):
            query_head, key_head, value_head, suffix_kh, suffix_vh, new_kh, new_vh = head_inputs
            prefix_scores = jnp.einsum('tsgd,ld->tsgl', query_head, key_head) * score_scale
            prefix_scores = jnp.where(visible, prefix_scores, MASKED)
            suffix_scores = jnp.einsum('tsgd,sud->tsgu', query_head, suffix_kh) * score_scale
            new_scores = jnp.einsum('tsgd,usd->tsgu', query_head, new_kh) * score_scale
            new_scores = jnp.where(causal, new_scores, MASKED)
            row_top = jnp.maximum(jnp.maximum(prefix_scores.max(-1), suffix_scores.max(-1)), new_scores.max(-1))[..., None]
            prefix_weights = rounded(jnp.where(visible, jnp.exp(prefix_scores - row_top), 0.0))
            suffix_weights = rounded(jnp.exp(suffix_scores - row_top))
            new_weights = rounded(jnp.where(causal, jnp.exp(new_scores - row_top), 0.0))
            numerator = jnp.einsum('tsgl,ld->tsgd', prefix_weights, value_head)
            numerator = numerator + jnp.einsum('tsgu,sud->tsgd', suffix_weights, suffix_vh)
            numerator = numerator + jnp.einsum('tsgu,usd->tsgd', new_weights, new_vh)
            denominator = prefix_weights.sum(-1) + suffix_weights.sum(-1) + new_weights.sum(-1)
            return numerator / denominator[..., None]
        return lax.map(one_head, (query_block, key_block, value_block, suffix_key, suffix_value, new_key, new_value))
    attended = lax.map(one_prompt, (query_sorted, prefix_key_heads, prefix_value_heads, suffix_key_sorted, suffix_value_sorted, new_key_sorted, new_value_sorted, prompt_lengths))
    attended = jnp.transpose(attended, (2, 0, 3, 1, 4, 5)).reshape(STEPS, SLOTS, HQ, HD)
    living = jnp.arange(SAMPLES, dtype=jnp.int32)[None, None, :] < unfinished[:, :, None]
    living = living.reshape(STEPS, SLOTS, 1, 1)
    attended = jnp.where(living, attended, 0.0)
    attended = jnp.take(attended, slot_sample, axis=1)
    return attended.astype(jnp.bfloat16)
```

```python
import math

import jax
import jax.numpy as jnp
import numpy as np
from jax import lax
from jax.experimental import pallas as pl
from jax.experimental.pallas import tpu as pltpu
from jax.sharding import PartitionSpec as P

SAMPLES = 16
MASKED = -1e30
ABSENT = -60000.0
F32 = jnp.float32
BF16 = jnp.bfloat16
TAKERS = [[(0, 0)], [(0, 1)], [(0, 2), (1, 0)], [(1, 1)], [(1, 2)],
          [(2, 0)], [(2, 1)], [(2, 2), (3, 0)], [(3, 1)], [(3, 2)]]
VMEM = pl.BlockSpec(memory_space=pltpu.VMEM)
SMEM = pl.BlockSpec(memory_space=pltpu.SMEM)
PARAMS = pltpu.CompilerParams(vmem_limit_bytes=40 * 1024 * 1024)


HBM = pl.BlockSpec(memory_space=pltpu.HBM)
HIGHEST = lax.Precision.HIGHEST


def send_kernel(core_ref, row_ref, slot_ref, slots_ref, k_hbm, v_hbm, q_hbm, out_hbm, mode_ref,
                k_ref, v_ref, q_ref, some_q, out_ref, list_ref, in_sem, out_sem):
    ins = []
    for n, (src, dst) in enumerate(((k_hbm, k_ref), (v_hbm, v_ref))):
        for i in range(2):
            part = pl.ds(i * 1280, 1280)
            ins.append(pltpu.make_async_copy(src.at[part], dst.at[part], in_sem.at[n * 2 + i]))
    ins.append(pltpu.make_async_copy(q_hbm, q_ref, in_sem.at[4]))
    for copy in ins:
        copy.start()
    outs = []
    for i in range(40):
        list_ref[i] = 0
    counts = [jnp.int32(0)] * 4
    for i in range(40):
        sample = slot_ref[row_ref[0] * 40 + i]
        to = (sample >= 40).astype(jnp.int32) + (sample >= 80).astype(jnp.int32) + (sample >= 120).astype(jnp.int32)
        n = jnp.where(to < 2, jnp.where(to == 0, counts[0], counts[1]), jnp.where(to == 2, counts[2], counts[3]))
        counts = [counts[k] + (to == k).astype(jnp.int32) for k in range(4)]
        mine = ((n & 1) == core_ref[0]) & (n < 20)
        list_ref[jnp.where(mine, to * 10 + (n >> 1), 40)] = i

    def quarter(a):
        return (a >= 40).astype(jnp.int32) + (a >= 80).astype(jnp.int32) + (a >= 120).astype(jnp.int32)

    pair = lax.broadcasted_iota(jnp.int32, (16, 160), 0)
    common = quarter(lax.broadcasted_iota(jnp.int32, (16, 160), 1)) * 4 + quarter(slots_ref[...])
    owed = jnp.sum(jnp.where(common == pair, 1.0, 0.0), axis=1, keepdims=True)
    mode_ref[0] = (jnp.max(owed) > 20.0).astype(jnp.int32)

    def leave(dst, at, size):
        rows = pl.ds(at, size)
        copy = pltpu.make_async_copy(out_ref.at[dst, rows], out_hbm.at[dst, rows], out_sem.at[len(outs)])
        copy.start()
        outs.append(copy)

    to = lax.broadcasted_iota(jnp.int32, (256, 256), 0)
    row = lax.broadcasted_iota(jnp.int32, (256, 256), 1)
    apart = jnp.where(row == (to % 128) * 2 + to // 128, 1.0, 0.0).astype(BF16)
    for n, ref in enumerate((k_ref, v_ref)):
        for i in range(2):
            ins[n * 2 + i].wait()
            for p in range(i * 5, i * 5 + 5):
                rows = jnp.dot(apart, ref[pl.ds(p * 256, 256), :], preferred_element_type=F32).astype(BF16)
                for h in range(2):
                    for y, b in TAKERS[p]:
                        out_ref[h * 4 + y, pl.ds(n * 384 + b * 128, 128), :] = rows[h * 128:h * 128 + 128]
            for dst in (2 * i, 2 * i + 1, 2 * i + 4, 2 * i + 5):
                leave(dst, n * 384, 384)
    ins[4].wait()
    for y in range(4):
        for i in range(10):
            slot = list_ref[y * 10 + i]
            for t in range(3):
                rows = q_ref[t, slot].astype(F32)
                for h in range(2):
                    some_q[h, y, t * 80 + i * 8:t * 80 + i * 8 + 8, :] = rows[h * 8:h * 8 + 8]
        for h in range(2):
            out_ref[h * 4 + y, pl.ds(768, 240), :] = some_q[h, y].astype(BF16)
            leave(h * 4 + y, 768, 240)
    for copy in outs:
        copy.wait()


def attend_kernel(mode_ref, block_ref, limit_ref, start_ref, met_ref, order_ref, heads_ref, extra_hbm,
                  o_ref, every_q, some_q, extra_ref, sem):
    @pl.when(mode_ref[0] == 0)
    def _():
        for src in range(8):
            every_q[pl.ds(src * 240, 240), :] = met_ref[src, pl.ds(768, 240), :].astype(F32)

    @pl.when(mode_ref[0] != 0)
    def _():
        copy = pltpu.make_async_copy(extra_hbm, extra_ref, sem)
        copy.start()
        copy.wait()
        every_q[...] = extra_ref[...].astype(F32)

    stride = jnp.where(mode_ref[0] == 0, 80, 160)
    order = order_ref[...]
    n = lax.broadcasted_iota(jnp.int32, (192, 128), 0)
    lane_of = (n // 96) * 64 + n % 12
    lanes = lax.broadcasted_iota(jnp.int32, (192, 128), 1)
    every_lse = jnp.zeros((8, 128), F32)
    for j in range(5):
        for r in range(8):
            start = start_ref[j * 8 + r]
            for t in range(3):
                row = pl.multiple_of(start + t * stride, 8)
                some_q[j, pl.ds((r * 3 + t) * 8, 8), :] = every_q[pl.ds(row, 8), :]
    for j in range(5):
        q = jnp.dot(order, some_q[j].astype(BF16), preferred_element_type=F32).astype(BF16)
        at = pl.multiple_of(block_ref[j] * 128, 128)
        k = met_ref[:, pl.ds(at, 128), :].reshape(1024, 128)
        v = met_ref[:, pl.ds(384 + at, 128), :].reshape(1024, 128)
        s = lax.dot_general(q, k, (((1,), (1,)), ((), ())), preferred_element_type=F32)
        seen = lax.broadcasted_iota(jnp.int32, s.shape, 1) < limit_ref[j]
        s = jnp.where(seen, s * (math.log2(math.e) / math.sqrt(128)), MASKED)
        top = jnp.max(s, axis=-1, keepdims=True)
        p = jnp.exp2(s - top)
        total = jnp.sum(p, axis=-1, keepdims=True)
        hi = p.astype(BF16)
        lo = (p - hi.astype(F32)).astype(BF16)
        o = jnp.dot(hi, v, preferred_element_type=F32)
        o = o + jnp.dot(lo, v, preferred_element_type=F32)
        some = limit_ref[j] > 0
        o = o / total
        low, high = o[:96], o[96:]
        for h, a in enumerate((jnp.concatenate([low[:, :64], high[:, :64]], axis=1),
                               jnp.concatenate([low[:, 64:], high[:, 64:]], axis=1))):
            for g in range(8):
                o_ref[2 * g + h, pl.ds(j * 12, 12), :] = a[g * 12:g * 12 + 12]
        lse = jnp.where(some, top * math.log(2.0) + jnp.log(total), ABSENT)
        spread = jnp.where(lanes == lane_of + j * 12, lse, 0.0)
        every_lse = every_lse + jnp.dot(heads_ref[...], spread, precision=HIGHEST, preferred_element_type=F32)
    a = every_lse.astype(BF16).astype(F32)
    rest = every_lse - a
    b = rest.astype(BF16).astype(F32)
    c = (rest - b).astype(BF16).astype(F32)
    for g in range(8):
        for h in range(2):
            o_ref[2 * g + h, 60:64, :] = jnp.concatenate(
                [a[g:g + 1], b[g:g + 1], c[g:g + 1], jnp.zeros((1, 128), F32)], axis=0)


def combine_kernel(got_ref, out_ref):
    lse = got_ref[:, 60, :] + got_ref[:, 61, :] + got_ref[:, 62, :]
    top = jnp.max(lse, axis=0, keepdims=True)
    w = jnp.exp(lse - top)
    total = jnp.sum(w, axis=0, keepdims=True)
    w = jnp.concatenate([w / total, jnp.zeros((112, 128), F32)], axis=0).T
    left = lax.broadcasted_iota(jnp.int32, (64, 128), 1) < 64
    o = jnp.zeros((64, 128), F32)
    for i in range(16):
        o = o + got_ref[i] * jnp.where(left, w[:64, i:i + 1], w[64:, i:i + 1])
    o = jnp.concatenate([o[:56], o[56:60], top + jnp.log(total), jnp.zeros((3, 128), F32)], axis=0)
    for i in range(4):
        out_ref[i] = o


def finish_kernel(every_ref, own_ref, num_ref, out_ref):
    flat = every_ref[...].reshape(256, 128)
    own = own_ref[...].T
    place = own[:, 0:1].astype(jnp.int32)
    lane = own[:, 1:2].astype(jnp.int32)
    half = own[:, 2:3]
    columns = lax.broadcasted_iota(jnp.int32, (128, 256), 1)
    pick = jnp.where(columns == place, 1.0, 0.0).astype(BF16)
    hi = flat.astype(BF16)
    lo = (flat - hi.astype(F32)).astype(BF16)
    o = jnp.dot(pick, hi, preferred_element_type=F32) + jnp.dot(pick, lo, preferred_element_type=F32)
    o = jnp.where(half == 0.0, o[:, :64], o[:, 64:])
    lanes = lax.broadcasted_iota(jnp.int32, (128, 128), 1)
    kept = jnp.zeros((128, 128), F32)
    for y in range(4):
        kept = jnp.where(lanes + y * 128 == lane, flat[y * 64 + 60:y * 64 + 61], kept)
    lse = jnp.sum(kept, axis=1, keepdims=True)
    own_top, den, living = own[:, 3:4], own[:, 4:5], own[:, 5:6]
    top = jnp.maximum(lse, own_top)
    a = jnp.exp(lse - top)
    b = jnp.exp(own_top - top)
    out = (a * o + b * num_ref[...]) / (a + b * den)
    out = jnp.where(living > 0.0, out, 0.0)
    out = jnp.concatenate([out[:64], out[64:]], axis=1).astype(BF16)
    for i in range(16):
        out_ref[i] = out


def lay(ref, to_ref, first):
    for g in range(8):
        left, right = ref[2 * g].astype(F32), ref[2 * g + 1].astype(F32)
        for k in range(2):
            cut = slice(k * 64, k * 64 + 64)
            rows = jnp.concatenate([left[:, cut], right[:, cut]], axis=1)
            for t in range(3):
                to_ref[t * 40 + k * 20:t * 40 + k * 20 + 20, first + g, :] = rows[t * 20:t * 20 + 20]


def own_lay_kernel(mine_ref, out_ref):
    lay(mine_ref, out_ref, 0)


def final_kernel(core_ref, mine_ref, other_ref, out_ref, whole):
    for core in range(2):
        @pl.when(core_ref[0] == core)
        def _():
            whole[:, core * 8:core * 8 + 8, :] = mine_ref[...]
            lay(other_ref, whole, 8 - core * 8)
    out_ref[...] = whole[...].reshape(3, 40, 16, 128).astype(BF16)


def shards(
    queries, prefix_keys, prefix_values, suffix_keys, suffix_values,
    new_keys, new_values, prompt_lengths, unfinished, slot_sample,
):
    steps, slots, heads, width = queries.shape
    prompts, span, key_heads, _ = prefix_keys.shape
    group = heads // key_heads
    scale = 1.0 / math.sqrt(width)
    pr = lax.axis_index("prompt")
    z, c = pr // 2, pr % 2
    y = lax.axis_index("sample")
    t_ids = jnp.arange(steps, dtype=jnp.int32)
    near = [list(range(8 * i, 8 * i + 8)) for i in range(16)]
    same_core = [[2 * i + k for i in range(16)] for k in range(2)]

    sent, mode = pl.pallas_call(
        send_kernel,
        in_specs=[SMEM, SMEM, SMEM, VMEM, HBM, HBM, HBM],
        out_specs=[HBM, SMEM],
        out_shape=[jax.ShapeDtypeStruct((8, 1008, 128), BF16), jax.ShapeDtypeStruct((1,), jnp.int32)],
        scratch_shapes=[
            pltpu.VMEM((2560, 128), BF16),
            pltpu.VMEM((2560, 128), BF16),
            pltpu.VMEM((3, 40, 16, 128), BF16),
            pltpu.VMEM((2, 4, 240, 128), F32),
            pltpu.VMEM((8, 1008, 128), BF16),
            pltpu.SMEM((48,), jnp.int32),
            pltpu.SemaphoreType.DMA((5,)),
            pltpu.SemaphoreType.DMA((24,)),
        ],
        compiler_params=pltpu.CompilerParams(vmem_limit_bytes=60 * 1024 * 1024),
    )(c.reshape(1).astype(jnp.int32), y.reshape(1).astype(jnp.int32), slot_sample, slot_sample.reshape(1, 160),
      prefix_keys.reshape(2560, width), prefix_values.reshape(2560, width), queries)
    met = lax.all_to_all(sent, ("prompt", "sample"), 0, 0, axis_index_groups=near, tiled=True)

    ids = jnp.arange(160, dtype=jnp.int32)
    wanted = y * slots + jnp.arange(slots, dtype=jnp.int32)
    slot_of = jnp.sum(jnp.where(slot_sample[None, :] == wanted[:, None], ids[None, :], 0), axis=1)
    at, from_row = slot_of % slots, slot_of // slots
    owner = slot_sample // slots
    ahead = (ids // slots == from_row[:, None]) & (ids < slot_of[:, None]) & (owner == y)
    rank = jnp.sum(ahead.astype(jnp.int32), axis=1)
    many = mode[0] > 0
    start = jnp.where(
        many,
        ((at // 20) * 4 + from_row) * 480 + (at % 20) * 8,
        ((rank % 2) * 4 + from_row) * 240 + (rank // 2) * 8,
    )

    def all_queries():
        half = lax.dynamic_slice_in_dim(queries, c * (slots // 2), slots // 2, 1)
        half = half.reshape(steps, slots // 2, key_heads, group, width)
        half = jnp.transpose(half, (2, 0, 1, 3, 4)).reshape(2, 1, 480, width)
        half = jnp.broadcast_to(half, (2, 4, 480, width)).reshape(8, 480, width)
        half = lax.all_to_all(half, ("prompt", "sample"), 0, 0, axis_index_groups=near, tiled=True)
        return half.reshape(3840, width)


    extra = lax.cond(many, all_queries, lambda: jnp.zeros((3840, width), BF16))

    odd = y % 2
    block = jnp.where(odd == 0, jnp.array([0, 0, 1, 1, 2], jnp.int32), jnp.array([0, 1, 1, 2, 2], jnp.int32))
    limit = jnp.take(prompt_lengths, (y * 5) // 2 + block) - z * 1024
    n = np.arange(192)
    order = np.zeros((192, 192), np.float32)
    order[n, ((n // 96) * 12 + n % 12) * 8 + (n % 96) // 12] = 1.0
    def rows(a):
        a = jnp.broadcast_to(a, (steps, slots) + a.shape[2:])
        a = a.reshape((steps, 2, 20) + a.shape[2:])
        a = jnp.swapaxes(a, 0, 1).reshape((2, 60) + a.shape[3:])
        return jnp.pad(a, [(0, 0), (0, 4)] + [(0, 0)] * (a.ndim - 2)).reshape((128,) + a.shape[2:])

    own_id = lax.dynamic_slice_in_dim(slot_sample, y * slots, slots, 0)
    from_y = (own_id // slots)[None, :]
    r = own_id % slots
    half = ((r % 8) // 4)[None, :]
    row = ((r // 8) * 12 + (r % 4) * 3)[None, :] + t_ids[:, None]
    going = jnp.take(unfinished, own_id // SAMPLES, axis=1)
    living = (own_id % SAMPLES)[None, :] < going
    place, lane = from_y * 64 + row, from_y * 128 + half * 64 + row

    qs = queries.reshape(steps, slots, key_heads, group, width)
    qs = lax.dynamic_slice(qs, (0, 0, c, z // 2, 0), (steps, slots, 1, 1, width))[:, :, 0, 0].astype(F32)

    def of_head(old, new, first, size):
        a = jnp.concatenate([old, jnp.swapaxes(new, 0, 1)], axis=1)
        return lax.dynamic_slice(a, (0, 0, c, first), a.shape[:2] + (1, size))[:, :, 0].astype(F32)

    keys = of_head(suffix_keys, new_keys, 0, width)
    values = of_head(suffix_values, new_values, (z % 2) * 64, 64)
    score = jnp.sum(qs[:, :, None] * keys[None], axis=-1) * scale
    u_ids = jnp.arange(keys.shape[1], dtype=jnp.int32)
    seen = (u_ids[None, :] <= suffix_keys.shape[1] + t_ids[:, None])[:, None, :]
    score = jnp.where(seen, score, MASKED)
    own_top = jnp.max(score, axis=2)
    weight = jnp.where(seen, jnp.exp(score - own_top[:, :, None]), 0.0)
    den = jnp.sum(weight, axis=2)
    num = jnp.sum(weight[..., None] * values[None], axis=2)
    own = jnp.stack([jnp.broadcast_to(a, (steps, slots)).astype(F32) for a in (place, lane, half, own_top, den, living)])
    own = jnp.swapaxes(own.reshape(6, steps, 2, 20), 1, 2).reshape(6, 2, 60)
    own = jnp.pad(own, ((0, 2), (0, 0), (0, 4))).reshape(8, 128)
    met, own, num, extra = lax.optimization_barrier((met, own, rows(num), extra))

    of_heads = np.zeros((8, 192), np.float32)
    of_heads[(n % 96) // 12, n] = 1.0
    part = pl.pallas_call(
        attend_kernel,
        in_specs=[SMEM, SMEM, SMEM, SMEM, VMEM, VMEM, VMEM, HBM],
        out_specs=VMEM,
        out_shape=jax.ShapeDtypeStruct((16, 64, 128), F32),
        scratch_shapes=[
            pltpu.VMEM((3840, 128), F32),
            pltpu.VMEM((5, 192, 128), F32),
            pltpu.VMEM((3840, 128), BF16),
            pltpu.SemaphoreType.DMA,
        ],
        compiler_params=PARAMS,
    )(many.astype(jnp.int32).reshape(1), block, limit, start, met, jnp.asarray(order, BF16), jnp.asarray(of_heads, F32), extra)

    got = lax.all_to_all(part.astype(jnp.float16), "prompt", 0, 0, axis_index_groups=same_core, tiled=True)

    part = pl.pallas_call(
        combine_kernel,
        in_specs=[VMEM],
        out_specs=VMEM,
        out_shape=jax.ShapeDtypeStruct((4, 64, 128), F32),
        compiler_params=PARAMS,
    )(got.astype(F32))
    every = lax.all_to_all(part, "sample", 0, 0, tiled=True)
    part = pl.pallas_call(
        finish_kernel,
        in_specs=[VMEM] * 3,
        out_specs=VMEM,
        out_shape=jax.ShapeDtypeStruct((16, 64, 128), BF16),
        compiler_params=PARAMS,
    )(every, own, num)

    mine = lax.all_to_all(part, "prompt", 0, 0, axis_index_groups=same_core, tiled=True)
    other = lax.ppermute(mine, "prompt", [(i, i ^ 1) for i in range(32)])
    mine = pl.pallas_call(
        own_lay_kernel,
        in_specs=[VMEM],
        out_specs=VMEM,
        out_shape=jax.ShapeDtypeStruct((120, 8, 128), F32),
        compiler_params=PARAMS,
        cost_estimate=pl.CostEstimate(flops=1000000, bytes_accessed=1500000, transcendentals=0),
    )(mine)
    return pl.pallas_call(
        final_kernel,
        in_specs=[SMEM, VMEM, VMEM],
        out_specs=VMEM,
        out_shape=jax.ShapeDtypeStruct((steps, slots, heads, width), BF16),
        scratch_shapes=[pltpu.VMEM((120, 16, 128), F32)],
        compiler_params=PARAMS,
    )(c.reshape(1).astype(jnp.int32), mine, other)


def solution(mesh):
    in_specs = (
        P(None, "sample", "tensor", None),
        P(None, ("prompt", "sample"), "tensor", None),
        P(None, ("prompt", "sample"), "tensor", None),
        P("sample", None, "tensor", None),
        P("sample", None, "tensor", None),
        P(None, "sample", "tensor", None),
        P(None, "sample", "tensor", None),
        P(),
        P(),
        P(),
    )
    out_specs = P(None, "sample", "tensor", None)
    return jax.shard_map(shards, mesh=mesh, in_specs=in_specs, out_specs=out_specs, check_vma=False)
```

```python
import math

import jax
import jax.numpy as jnp
import numpy as np
from jax import lax
from jax.experimental import pallas as pl
from jax.experimental.pallas import tpu as pltpu
from jax.sharding import PartitionSpec as P

SAMPLES = 16
MASKED = -1e30
ABSENT = -60000.0
F32 = jnp.float32
BF16 = jnp.bfloat16
TAKERS = [[(0, 0)], [(0, 1)], [(0, 2), (1, 0)], [(1, 1)], [(1, 2)],
          [(2, 0)], [(2, 1)], [(2, 2), (3, 0)], [(3, 1)], [(3, 2)]]
VMEM = pl.BlockSpec(memory_space=pltpu.VMEM)
SMEM = pl.BlockSpec(memory_space=pltpu.SMEM)
PARAMS = pltpu.CompilerParams(vmem_limit_bytes=40 * 1024 * 1024)


HBM = pl.BlockSpec(memory_space=pltpu.HBM)
HIGHEST = lax.Precision.HIGHEST


def send_kernel(core_ref, row_ref, slot_ref, slots_ref, k_hbm, v_hbm, q_hbm, out_hbm, mode_ref,
                k_ref, v_ref, q_ref, some_q, out_ref, list_ref, count_ref, in_sem, out_sem):
    ins = []
    for n, (src, dst) in enumerate(((k_hbm, k_ref), (v_hbm, v_ref))):
        for i in range(2):
            part = pl.ds(i * 1280, 1280)
            ins.append(pltpu.make_async_copy(src.at[part], dst.at[part], in_sem.at[n * 2 + i]))
    ins.append(pltpu.make_async_copy(q_hbm, q_ref, in_sem.at[4]))
    for copy in ins:
        copy.start()
    outs = []
    for i in range(40):
        list_ref[i] = 0
    for i in range(4):
        count_ref[i] = 0

    def note(i, _):
        sample = slot_ref[row_ref[0] * 40 + i]
        to = (sample >= 40).astype(jnp.int32) + (sample >= 80).astype(jnp.int32) + (sample >= 120).astype(jnp.int32)
        n = count_ref[to]
        count_ref[to] = n + 1

        @pl.when(((n & 1) == core_ref[0]) & (n < 20))
        def _():
            list_ref[to * 10 + (n >> 1)] = i
        return 0

    lax.fori_loop(0, 40, note, 0)

    def quarter(a):
        return (a >= 40).astype(jnp.int32) + (a >= 80).astype(jnp.int32) + (a >= 120).astype(jnp.int32)

    pair = lax.broadcasted_iota(jnp.int32, (16, 160), 0)
    common = quarter(lax.broadcasted_iota(jnp.int32, (16, 160), 1)) * 4 + quarter(slots_ref[...])
    owed = jnp.sum(jnp.where(common == pair, 1.0, 0.0), axis=1, keepdims=True)
    mode_ref[0] = (jnp.max(owed) > 20.0).astype(jnp.int32)

    def leave(dst, at, size):
        rows = pl.ds(at, size)
        copy = pltpu.make_async_copy(out_ref.at[dst, rows], out_hbm.at[dst, rows], out_sem.at[len(outs)])
        copy.start()
        outs.append(copy)

    to = lax.broadcasted_iota(jnp.int32, (256, 256), 0)
    row = lax.broadcasted_iota(jnp.int32, (256, 256), 1)
    apart = jnp.where(row == (to % 128) * 2 + to // 128, 1.0, 0.0).astype(BF16)
    for n, ref in enumerate((k_ref, v_ref)):
        for i in range(2):
            ins[n * 2 + i].wait()
            for p in range(i * 5, i * 5 + 5):
                rows = jnp.dot(apart, ref[pl.ds(p * 256, 256), :], preferred_element_type=F32).astype(BF16)
                for h in range(2):
                    for y, b in TAKERS[p]:
                        out_ref[h * 4 + y, pl.ds(n * 384 + b * 128, 128), :] = rows[h * 128:h * 128 + 128]
            for dst in (2 * i, 2 * i + 1, 2 * i + 4, 2 * i + 5):
                leave(dst, n * 384, 384)
    ins[4].wait()
    for y in range(4):
        for i in range(10):
            slot = list_ref[y * 10 + i]
            for t in range(3):
                rows = q_ref[t, slot].astype(F32)
                for h in range(2):
                    some_q[h, y, t * 80 + i * 8:t * 80 + i * 8 + 8, :] = rows[h * 8:h * 8 + 8]
        for h in range(2):
            out_ref[h * 4 + y, pl.ds(768, 240), :] = some_q[h, y].astype(BF16)
            leave(h * 4 + y, 768, 240)
    for copy in outs:
        copy.wait()


def attend_kernel(mode_ref, block_ref, limit_ref, start_ref, met_ref, order_ref, heads_ref, extra_hbm,
                  o_ref, every_q, some_q, extra_ref, sem):
    @pl.when(mode_ref[0] == 0)
    def _():
        for src in range(8):
            every_q[pl.ds(src * 240, 240), :] = met_ref[src, pl.ds(768, 240), :].astype(F32)

    @pl.when(mode_ref[0] != 0)
    def _():
        copy = pltpu.make_async_copy(extra_hbm, extra_ref, sem)
        copy.start()
        copy.wait()
        every_q[...] = extra_ref[...].astype(F32)

    stride = jnp.where(mode_ref[0] == 0, 80, 160)
    order = order_ref[...]
    n = lax.broadcasted_iota(jnp.int32, (192, 128), 0)
    lane_of = (n // 96) * 64 + n % 12
    lanes = lax.broadcasted_iota(jnp.int32, (192, 128), 1)
    every_lse = jnp.zeros((8, 128), F32)
    for j in range(5):
        for r in range(8):
            start = start_ref[j * 8 + r]
            for t in range(3):
                row = pl.multiple_of(start + t * stride, 8)
                some_q[j, pl.ds((r * 3 + t) * 8, 8), :] = every_q[pl.ds(row, 8), :]
    for j in range(5):
        q = jnp.dot(order, some_q[j].astype(BF16), preferred_element_type=F32).astype(BF16)
        at = pl.multiple_of(block_ref[j] * 128, 128)
        k = met_ref[:, pl.ds(at, 128), :].reshape(1024, 128)
        v = met_ref[:, pl.ds(384 + at, 128), :].reshape(1024, 128)
        s = lax.dot_general(q, k, (((1,), (1,)), ((), ())), preferred_element_type=F32)
        seen = lax.broadcasted_iota(jnp.int32, s.shape, 1) < limit_ref[j]
        s = jnp.where(seen, s * (math.log2(math.e) / math.sqrt(128)), MASKED)
        top = jnp.max(s, axis=-1, keepdims=True)
        p = jnp.exp2(s - top)
        total = jnp.sum(p, axis=-1, keepdims=True)
        hi = p.astype(BF16)
        lo = (p - hi.astype(F32)).astype(BF16)
        o = jnp.dot(hi, v, preferred_element_type=F32)
        o = o + jnp.dot(lo, v, preferred_element_type=F32)
        some = limit_ref[j] > 0
        o = o / total
        low, high = o[:96], o[96:]
        for h, a in enumerate((jnp.concatenate([low[:, :64], high[:, :64]], axis=1),
                               jnp.concatenate([low[:, 64:], high[:, 64:]], axis=1))):
            for g in range(8):
                o_ref[2 * g + h, pl.ds(j * 12, 12), :] = a[g * 12:g * 12 + 12]
        lse = jnp.where(some, top * math.log(2.0) + jnp.log(total), ABSENT)
        spread = jnp.where(lanes == lane_of + j * 12, lse, 0.0)
        every_lse = every_lse + jnp.dot(heads_ref[...], spread, precision=HIGHEST, preferred_element_type=F32)
    a = every_lse.astype(BF16).astype(F32)
    rest = every_lse - a
    b = rest.astype(BF16).astype(F32)
    c = (rest - b).astype(BF16).astype(F32)
    for g in range(8):
        for h in range(2):
            o_ref[2 * g + h, 60:64, :] = jnp.concatenate(
                [a[g:g + 1], b[g:g + 1], c[g:g + 1], jnp.zeros((1, 128), F32)], axis=0)


def combine_kernel(got_ref, out_ref):
    lse = got_ref[:, 60, :] + got_ref[:, 61, :] + got_ref[:, 62, :]
    top = jnp.max(lse, axis=0, keepdims=True)
    w = jnp.exp(lse - top)
    total = jnp.sum(w, axis=0, keepdims=True)
    w = jnp.concatenate([w / total, jnp.zeros((112, 128), F32)], axis=0).T
    left = lax.broadcasted_iota(jnp.int32, (64, 128), 1) < 64
    o = jnp.zeros((64, 128), F32)
    for i in range(16):
        o = o + got_ref[i] * jnp.where(left, w[:64, i:i + 1], w[64:, i:i + 1])
    o = jnp.concatenate([o[:56], o[56:60], top + jnp.log(total), jnp.zeros((3, 128), F32)], axis=0)
    for i in range(4):
        out_ref[i] = o


def finish_kernel(every_ref, own_ref, num_ref, out_ref):
    flat = every_ref[...].reshape(256, 128)
    own = own_ref[...].T
    place = own[:, 0:1].astype(jnp.int32)
    lane = own[:, 1:2].astype(jnp.int32)
    half = own[:, 2:3]
    columns = lax.broadcasted_iota(jnp.int32, (128, 256), 1)
    pick = jnp.where(columns == place, 1.0, 0.0).astype(BF16)
    hi = flat.astype(BF16)
    lo = (flat - hi.astype(F32)).astype(BF16)
    o = jnp.dot(pick, hi, preferred_element_type=F32) + jnp.dot(pick, lo, preferred_element_type=F32)
    o = jnp.where(half == 0.0, o[:, :64], o[:, 64:])
    lanes = lax.broadcasted_iota(jnp.int32, (128, 128), 1)
    kept = jnp.zeros((128, 128), F32)
    for y in range(4):
        kept = jnp.where(lanes + y * 128 == lane, flat[y * 64 + 60:y * 64 + 61], kept)
    lse = jnp.sum(kept, axis=1, keepdims=True)
    own_top, den, living = own[:, 3:4], own[:, 4:5], own[:, 5:6]
    top = jnp.maximum(lse, own_top)
    a = jnp.exp(lse - top)
    b = jnp.exp(own_top - top)
    out = (a * o + b * num_ref[...]) / (a + b * den)
    out = jnp.where(living > 0.0, out, 0.0)
    out = jnp.concatenate([out[:64], out[64:]], axis=1).astype(BF16)
    for i in range(16):
        out_ref[i] = out


def lay(ref, to_ref, first):
    for g in range(8):
        left, right = ref[2 * g].astype(F32), ref[2 * g + 1].astype(F32)
        for k in range(2):
            cut = slice(k * 64, k * 64 + 64)
            rows = jnp.concatenate([left[:, cut], right[:, cut]], axis=1)
            for t in range(3):
                to_ref[t * 40 + k * 20:t * 40 + k * 20 + 20, first + g, :] = rows[t * 20:t * 20 + 20]


def own_lay_kernel(mine_ref, out_ref):
    lay(mine_ref, out_ref, 0)


def final_kernel(core_ref, mine_ref, other_ref, out_ref, whole):
    for core in range(2):
        @pl.when(core_ref[0] == core)
        def _():
            whole[:, core * 8:core * 8 + 8, :] = mine_ref[...]
            lay(other_ref, whole, 8 - core * 8)
    out_ref[...] = whole[...].reshape(3, 40, 16, 128).astype(BF16)


def shards(
    queries, prefix_keys, prefix_values, suffix_keys, suffix_values,
    new_keys, new_values, prompt_lengths, unfinished, slot_sample,
):
    steps, slots, heads, width = queries.shape
    prompts, span, key_heads, _ = prefix_keys.shape
    group = heads // key_heads
    scale = 1.0 / math.sqrt(width)
    pr = lax.axis_index("prompt")
    z, c = pr // 2, pr % 2
    y = lax.axis_index("sample")
    t_ids = jnp.arange(steps, dtype=jnp.int32)
    near = [list(range(8 * i, 8 * i + 8)) for i in range(16)]
    same_core = [[2 * i + k for i in range(16)] for k in range(2)]

    sent, mode = pl.pallas_call(
        send_kernel,
        in_specs=[SMEM, SMEM, SMEM, VMEM, HBM, HBM, HBM],
        out_specs=[HBM, SMEM],
        out_shape=[jax.ShapeDtypeStruct((8, 1008, 128), BF16), jax.ShapeDtypeStruct((1,), jnp.int32)],
        scratch_shapes=[
            pltpu.VMEM((2560, 128), BF16),
            pltpu.VMEM((2560, 128), BF16),
            pltpu.VMEM((3, 40, 16, 128), BF16),
            pltpu.VMEM((2, 4, 240, 128), F32),
            pltpu.VMEM((8, 1008, 128), BF16),
            pltpu.SMEM((40,), jnp.int32),
            pltpu.SMEM((4,), jnp.int32),
            pltpu.SemaphoreType.DMA((5,)),
            pltpu.SemaphoreType.DMA((24,)),
        ],
        compiler_params=pltpu.CompilerParams(vmem_limit_bytes=60 * 1024 * 1024),
    )(c.reshape(1).astype(jnp.int32), y.reshape(1).astype(jnp.int32), slot_sample, slot_sample.reshape(1, 160),
      prefix_keys.reshape(2560, width), prefix_values.reshape(2560, width), queries)
    met = lax.all_to_all(sent, ("prompt", "sample"), 0, 0, axis_index_groups=near, tiled=True)

    ids = jnp.arange(160, dtype=jnp.int32)
    wanted = y * slots + jnp.arange(slots, dtype=jnp.int32)
    slot_of = jnp.sum(jnp.where(slot_sample[None, :] == wanted[:, None], ids[None, :], 0), axis=1)
    at, from_row = slot_of % slots, slot_of // slots
    owner = slot_sample // slots
    ahead = (ids // slots == from_row[:, None]) & (ids < slot_of[:, None]) & (owner == y)
    rank = jnp.sum(ahead.astype(jnp.int32), axis=1)
    many = mode[0] > 0
    start = jnp.where(
        many,
        ((at // 20) * 4 + from_row) * 480 + (at % 20) * 8,
        ((rank % 2) * 4 + from_row) * 240 + (rank // 2) * 8,
    )

    def all_queries():
        half = lax.dynamic_slice_in_dim(queries, c * (slots // 2), slots // 2, 1)
        half = half.reshape(steps, slots // 2, key_heads, group, width)
        half = jnp.transpose(half, (2, 0, 1, 3, 4)).reshape(2, 1, 480, width)
        half = jnp.broadcast_to(half, (2, 4, 480, width)).reshape(8, 480, width)
        half = lax.all_to_all(half, ("prompt", "sample"), 0, 0, axis_index_groups=near, tiled=True)
        return half.reshape(3840, width)


    extra = lax.cond(many, all_queries, lambda: jnp.zeros((3840, width), BF16))

    odd = y % 2
    block = jnp.where(odd == 0, jnp.array([0, 0, 1, 1, 2], jnp.int32), jnp.array([0, 1, 1, 2, 2], jnp.int32))
    limit = jnp.take(prompt_lengths, (y * 5) // 2 + block) - z * 1024
    n = np.arange(192)
    order = np.zeros((192, 192), np.float32)
    order[n, ((n // 96) * 12 + n % 12) * 8 + (n % 96) // 12] = 1.0
    def rows(a):
        a = jnp.broadcast_to(a, (steps, slots) + a.shape[2:])
        a = a.reshape((steps, 2, 20) + a.shape[2:])
        a = jnp.swapaxes(a, 0, 1).reshape((2, 60) + a.shape[3:])
        return jnp.pad(a, [(0, 0), (0, 4)] + [(0, 0)] * (a.ndim - 2)).reshape((128,) + a.shape[2:])

    own_id = lax.dynamic_slice_in_dim(slot_sample, y * slots, slots, 0)
    from_y = (own_id // slots)[None, :]
    r = own_id % slots
    half = ((r % 8) // 4)[None, :]
    row = ((r // 8) * 12 + (r % 4) * 3)[None, :] + t_ids[:, None]
    going = jnp.take(unfinished, own_id // SAMPLES, axis=1)
    living = (own_id % SAMPLES)[None, :] < going
    place, lane = from_y * 64 + row, from_y * 128 + half * 64 + row

    qs = queries.reshape(steps, slots, key_heads, group, width)
    qs = lax.dynamic_slice(qs, (0, 0, c, z // 2, 0), (steps, slots, 1, 1, width))[:, :, 0, 0].astype(F32)

    def of_head(old, new, first, size):
        a = jnp.concatenate([old, jnp.swapaxes(new, 0, 1)], axis=1)
        return lax.dynamic_slice(a, (0, 0, c, first), a.shape[:2] + (1, size))[:, :, 0].astype(F32)

    keys = of_head(suffix_keys, new_keys, 0, width)
    values = of_head(suffix_values, new_values, (z % 2) * 64, 64)
    score = jnp.sum(qs[:, :, None] * keys[None], axis=-1) * scale
    u_ids = jnp.arange(keys.shape[1], dtype=jnp.int32)
    seen = (u_ids[None, :] <= suffix_keys.shape[1] + t_ids[:, None])[:, None, :]
    score = jnp.where(seen, score, MASKED)
    own_top = jnp.max(score, axis=2)
    weight = jnp.where(seen, jnp.exp(score - own_top[:, :, None]), 0.0)
    den = jnp.sum(weight, axis=2)
    num = jnp.sum(weight[..., None] * values[None], axis=2)
    own = jnp.stack([jnp.broadcast_to(a, (steps, slots)).astype(F32) for a in (place, lane, half, own_top, den, living)])
    own = jnp.swapaxes(own.reshape(6, steps, 2, 20), 1, 2).reshape(6, 2, 60)
    own = jnp.pad(own, ((0, 2), (0, 0), (0, 4))).reshape(8, 128)
    met, own, num, extra = lax.optimization_barrier((met, own, rows(num), extra))

    of_heads = np.zeros((8, 192), np.float32)
    of_heads[(n % 96) // 12, n] = 1.0
    part = pl.pallas_call(
        attend_kernel,
        in_specs=[SMEM, SMEM, SMEM, SMEM, VMEM, VMEM, VMEM, HBM],
        out_specs=VMEM,
        out_shape=jax.ShapeDtypeStruct((16, 64, 128), F32),
        scratch_shapes=[
            pltpu.VMEM((3840, 128), F32),
            pltpu.VMEM((5, 192, 128), F32),
            pltpu.VMEM((3840, 128), BF16),
            pltpu.SemaphoreType.DMA,
        ],
        compiler_params=PARAMS,
    )(many.astype(jnp.int32).reshape(1), block, limit, start, met, jnp.asarray(order, BF16), jnp.asarray(of_heads, F32), extra)

    got = lax.all_to_all(part.astype(jnp.float16), "prompt", 0, 0, axis_index_groups=same_core, tiled=True)

    part = pl.pallas_call(
        combine_kernel,
        in_specs=[VMEM],
        out_specs=VMEM,
        out_shape=jax.ShapeDtypeStruct((4, 64, 128), F32),
        compiler_params=PARAMS,
    )(got.astype(F32))
    every = lax.all_to_all(part, "sample", 0, 0, tiled=True)
    part = pl.pallas_call(
        finish_kernel,
        in_specs=[VMEM] * 3,
        out_specs=VMEM,
        out_shape=jax.ShapeDtypeStruct((16, 64, 128), BF16),
        compiler_params=PARAMS,
    )(every, own, num)

    mine = lax.all_to_all(part, "prompt", 0, 0, axis_index_groups=same_core, tiled=True)
    other = lax.ppermute(mine, "prompt", [(i, i ^ 1) for i in range(32)])
    mine = pl.pallas_call(
        own_lay_kernel,
        in_specs=[VMEM],
        out_specs=VMEM,
        out_shape=jax.ShapeDtypeStruct((120, 8, 128), F32),
        compiler_params=PARAMS,
        cost_estimate=pl.CostEstimate(flops=1000000, bytes_accessed=1500000, transcendentals=0),
    )(mine)
    return pl.pallas_call(
        final_kernel,
        in_specs=[SMEM, VMEM, VMEM],
        out_specs=VMEM,
        out_shape=jax.ShapeDtypeStruct((steps, slots, heads, width), BF16),
        scratch_shapes=[pltpu.VMEM((120, 16, 128), F32)],
        compiler_params=PARAMS,
    )(c.reshape(1).astype(jnp.int32), mine, other)


def solution(mesh):
    in_specs = (
        P(None, "sample", "tensor", None),
        P(None, ("prompt", "sample"), "tensor", None),
        P(None, ("prompt", "sample"), "tensor", None),
        P("sample", None, "tensor", None),
        P("sample", None, "tensor", None),
        P(None, "sample", "tensor", None),
        P(None, "sample", "tensor", None),
        P(),
        P(),
        P(),
    )
    out_specs = P(None, "sample", "tensor", None)
    return jax.shard_map(shards, mesh=mesh, in_specs=in_specs, out_specs=out_specs, check_vma=False)
```

```python
import math

import jax
import jax.numpy as jnp
import numpy as np
from jax import lax
from jax.experimental import pallas as pl
from jax.experimental.pallas import tpu as pltpu
from jax.sharding import PartitionSpec as P

SAMPLES = 16
MASKED = -1e30
ABSENT = -60000.0
F32 = jnp.float32
BF16 = jnp.bfloat16
TAKERS = [[(0, 0)], [(0, 1)], [(0, 2), (1, 0)], [(1, 1)], [(1, 2)],
          [(2, 0)], [(2, 1)], [(2, 2), (3, 0)], [(3, 1)], [(3, 2)]]
VMEM = pl.BlockSpec(memory_space=pltpu.VMEM)
SMEM = pl.BlockSpec(memory_space=pltpu.SMEM)
PARAMS = pltpu.CompilerParams(vmem_limit_bytes=40 * 1024 * 1024)


HBM = pl.BlockSpec(memory_space=pltpu.HBM)
HIGHEST = lax.Precision.HIGHEST


def send_kernel(core_ref, row_ref, slot_ref, slots_ref, k_hbm, v_hbm, q_hbm, out_hbm, mode_ref,
                k_ref, v_ref, q_ref, some_q, out_ref, list_ref, count_ref, in_sem, out_sem):
    ins = []
    for n, (src, dst) in enumerate(((k_hbm, k_ref), (v_hbm, v_ref))):
        for i in range(2):
            part = pl.ds(i * 1280, 1280)
            ins.append(pltpu.make_async_copy(src.at[part], dst.at[part], in_sem.at[n * 2 + i]))
    ins.append(pltpu.make_async_copy(q_hbm, q_ref, in_sem.at[4]))
    for copy in ins:
        copy.start()
    outs = []
    for i in range(40):
        list_ref[i] = 0
    for i in range(4):
        count_ref[i] = 0

    def note(i, _):
        sample = slot_ref[row_ref[0] * 40 + i]
        to = (sample >= 40).astype(jnp.int32) + (sample >= 80).astype(jnp.int32) + (sample >= 120).astype(jnp.int32)
        n = count_ref[to]
        count_ref[to] = n + 1

        @pl.when(((n & 1) == core_ref[0]) & (n < 20))
        def _():
            list_ref[to * 10 + (n >> 1)] = i
        return 0

    lax.fori_loop(0, 40, note, 0)

    def quarter(a):
        return (a >= 40).astype(jnp.int32) + (a >= 80).astype(jnp.int32) + (a >= 120).astype(jnp.int32)

    pair = lax.broadcasted_iota(jnp.int32, (16, 160), 0)
    common = quarter(lax.broadcasted_iota(jnp.int32, (16, 160), 1)) * 4 + quarter(slots_ref[...])
    owed = jnp.sum(jnp.where(common == pair, 1.0, 0.0), axis=1, keepdims=True)
    mode_ref[0] = (jnp.max(owed) > 20.0).astype(jnp.int32)

    def leave(dst, at, size):
        rows = pl.ds(at, size)
        copy = pltpu.make_async_copy(out_ref.at[dst, rows], out_hbm.at[dst, rows], out_sem.at[len(outs)])
        copy.start()
        outs.append(copy)

    to = lax.broadcasted_iota(jnp.int32, (256, 256), 0)
    row = lax.broadcasted_iota(jnp.int32, (256, 256), 1)
    apart = jnp.where(row == (to % 128) * 2 + to // 128, 1.0, 0.0).astype(BF16)
    for n, ref in enumerate((k_ref, v_ref)):
        for i in range(2):
            ins[n * 2 + i].wait()
            for p in range(i * 5, i * 5 + 5):
                rows = jnp.dot(apart, ref[pl.ds(p * 256, 256), :], preferred_element_type=F32).astype(BF16)
                for h in range(2):
                    for y, b in TAKERS[p]:
                        out_ref[h * 4 + y, pl.ds(n * 384 + b * 128, 128), :] = rows[h * 128:h * 128 + 128]
            for dst in (2 * i, 2 * i + 1, 2 * i + 4, 2 * i + 5):
                leave(dst, n * 384, 384)
    ins[4].wait()
    for y in range(4):
        for i in range(10):
            slot = list_ref[y * 10 + i]
            for t in range(3):
                rows = q_ref[t, slot].astype(F32)
                for h in range(2):
                    some_q[h, y, t * 80 + i * 8:t * 80 + i * 8 + 8, :] = rows[h * 8:h * 8 + 8]
        for h in range(2):
            out_ref[h * 4 + y, pl.ds(768, 240), :] = some_q[h, y].astype(BF16)
            leave(h * 4 + y, 768, 240)
    for copy in outs:
        copy.wait()


def attend_kernel(mode_ref, block_ref, limit_ref, start_ref, met_ref, order_ref, heads_ref, extra_hbm,
                  o_ref, every_q, some_q, extra_ref, sem):
    @pl.when(mode_ref[0] == 0)
    def _():
        for src in range(8):
            every_q[pl.ds(src * 240, 240), :] = met_ref[src, pl.ds(768, 240), :].astype(F32)

    @pl.when(mode_ref[0] != 0)
    def _():
        copy = pltpu.make_async_copy(extra_hbm, extra_ref, sem)
        copy.start()
        copy.wait()
        every_q[...] = extra_ref[...].astype(F32)

    stride = jnp.where(mode_ref[0] == 0, 80, 160)
    order = order_ref[...]
    n = lax.broadcasted_iota(jnp.int32, (192, 128), 0)
    lane_of = (n // 96) * 64 + n % 12
    lanes = lax.broadcasted_iota(jnp.int32, (192, 128), 1)
    every_lse = jnp.zeros((8, 128), F32)
    for j in range(5):
        for r in range(8):
            start = start_ref[j * 8 + r]
            for t in range(3):
                row = pl.multiple_of(start + t * stride, 8)
                some_q[j, pl.ds((r * 3 + t) * 8, 8), :] = every_q[pl.ds(row, 8), :]
    for j in range(5):
        q = jnp.dot(order, some_q[j].astype(BF16), preferred_element_type=F32).astype(BF16)
        at = pl.multiple_of(block_ref[j] * 128, 128)
        k = met_ref[:, pl.ds(at, 128), :].reshape(1024, 128)
        v = met_ref[:, pl.ds(384 + at, 128), :].reshape(1024, 128)
        s = lax.dot_general(q, k, (((1,), (1,)), ((), ())), preferred_element_type=F32)
        unseen = jnp.where(lax.broadcasted_iota(jnp.int32, (1, 1024), 1) < limit_ref[j], 0.0, MASKED)
        s = s * (math.log2(math.e) / math.sqrt(128)) + unseen
        top = jnp.max(s, axis=-1, keepdims=True)
        p = jnp.exp2(s - top)
        total = jnp.sum(p, axis=-1, keepdims=True)
        hi = p.astype(BF16)
        lo = (p - hi.astype(F32)).astype(BF16)
        o = jnp.dot(hi, v, preferred_element_type=F32)
        o = o + jnp.dot(lo, v, preferred_element_type=F32)
        some = limit_ref[j] > 0
        o = o * (1.0 / total)
        low, high = o[:96], o[96:]
        for h, a in enumerate((jnp.concatenate([low[:, :64], high[:, :64]], axis=1),
                               jnp.concatenate([low[:, 64:], high[:, 64:]], axis=1))):
            for g in range(8):
                o_ref[2 * g + h, pl.ds(j * 12, 12), :] = a[g * 12:g * 12 + 12]
        lse = jnp.where(some, top * math.log(2.0) + jnp.log(total), ABSENT)
        spread = jnp.where(lanes == lane_of + j * 12, lse, 0.0)
        every_lse = every_lse + jnp.dot(heads_ref[...], spread, precision=HIGHEST, preferred_element_type=F32)
    a = every_lse.astype(BF16).astype(F32)
    rest = every_lse - a
    b = rest.astype(BF16).astype(F32)
    c = (rest - b).astype(BF16).astype(F32)
    for g in range(8):
        for h in range(2):
            o_ref[2 * g + h, 60:64, :] = jnp.concatenate(
                [a[g:g + 1], b[g:g + 1], c[g:g + 1], jnp.zeros((1, 128), F32)], axis=0)


def combine_kernel(got_ref, out_ref):
    lse = got_ref[:, 60, :] + got_ref[:, 61, :] + got_ref[:, 62, :]
    top = jnp.max(lse, axis=0, keepdims=True)
    w = jnp.exp(lse - top)
    total = jnp.sum(w, axis=0, keepdims=True)
    w = jnp.concatenate([w / total, jnp.zeros((112, 128), F32)], axis=0).T
    left = lax.broadcasted_iota(jnp.int32, (64, 128), 1) < 64
    o = jnp.zeros((64, 128), F32)
    for i in range(16):
        o = o + got_ref[i] * jnp.where(left, w[:64, i:i + 1], w[64:, i:i + 1])
    o = jnp.concatenate([o[:56], o[56:60], top + jnp.log(total), jnp.zeros((3, 128), F32)], axis=0)
    for i in range(4):
        out_ref[i] = o


def finish_kernel(every_ref, own_ref, num_ref, out_ref):
    flat = every_ref[...].reshape(256, 128)
    own = own_ref[...].T
    place = own[:, 0:1].astype(jnp.int32)
    lane = own[:, 1:2].astype(jnp.int32)
    half = own[:, 2:3]
    columns = lax.broadcasted_iota(jnp.int32, (128, 256), 1)
    pick = jnp.where(columns == place, 1.0, 0.0).astype(BF16)
    hi = flat.astype(BF16)
    lo = (flat - hi.astype(F32)).astype(BF16)
    o = jnp.dot(pick, hi, preferred_element_type=F32) + jnp.dot(pick, lo, preferred_element_type=F32)
    o = jnp.where(half == 0.0, o[:, :64], o[:, 64:])
    lanes = lax.broadcasted_iota(jnp.int32, (128, 128), 1)
    kept = jnp.zeros((128, 128), F32)
    for y in range(4):
        kept = jnp.where(lanes + y * 128 == lane, flat[y * 64 + 60:y * 64 + 61], kept)
    lse = jnp.sum(kept, axis=1, keepdims=True)
    own_top, den, living = own[:, 3:4], own[:, 4:5], own[:, 5:6]
    top = jnp.maximum(lse, own_top)
    a = jnp.exp(lse - top)
    b = jnp.exp(own_top - top)
    out = (a * o + b * num_ref[...]) / (a + b * den)
    out = jnp.where(living > 0.0, out, 0.0)
    out = jnp.concatenate([out[:64], out[64:]], axis=1).astype(BF16)
    for i in range(16):
        out_ref[i] = out


def lay(ref, to_ref, first):
    for g in range(8):
        left, right = ref[2 * g].astype(F32), ref[2 * g + 1].astype(F32)
        for k in range(2):
            cut = slice(k * 64, k * 64 + 64)
            rows = jnp.concatenate([left[:, cut], right[:, cut]], axis=1)
            for t in range(3):
                to_ref[t * 40 + k * 20:t * 40 + k * 20 + 20, first + g, :] = rows[t * 20:t * 20 + 20]


def own_lay_kernel(mine_ref, out_ref):
    lay(mine_ref, out_ref, 0)


def final_kernel(core_ref, mine_ref, other_ref, out_ref, whole):
    for core in range(2):
        @pl.when(core_ref[0] == core)
        def _():
            whole[:, core * 8:core * 8 + 8, :] = mine_ref[...]
            lay(other_ref, whole, 8 - core * 8)
    out_ref[...] = whole[...].reshape(3, 40, 16, 128).astype(BF16)


def shards(
    queries, prefix_keys, prefix_values, suffix_keys, suffix_values,
    new_keys, new_values, prompt_lengths, unfinished, slot_sample,
):
    steps, slots, heads, width = queries.shape
    prompts, span, key_heads, _ = prefix_keys.shape
    group = heads // key_heads
    scale = 1.0 / math.sqrt(width)
    pr = lax.axis_index("prompt")
    z, c = pr // 2, pr % 2
    y = lax.axis_index("sample")
    t_ids = jnp.arange(steps, dtype=jnp.int32)
    near = [list(range(8 * i, 8 * i + 8)) for i in range(16)]
    same_core = [[2 * i + k for i in range(16)] for k in range(2)]

    sent, mode = pl.pallas_call(
        send_kernel,
        in_specs=[SMEM, SMEM, SMEM, VMEM, HBM, HBM, HBM],
        out_specs=[HBM, SMEM],
        out_shape=[jax.ShapeDtypeStruct((8, 1008, 128), BF16), jax.ShapeDtypeStruct((1,), jnp.int32)],
        scratch_shapes=[
            pltpu.VMEM((2560, 128), BF16),
            pltpu.VMEM((2560, 128), BF16),
            pltpu.VMEM((3, 40, 16, 128), BF16),
            pltpu.VMEM((2, 4, 240, 128), F32),
            pltpu.VMEM((8, 1008, 128), BF16),
            pltpu.SMEM((40,), jnp.int32),
            pltpu.SMEM((4,), jnp.int32),
            pltpu.SemaphoreType.DMA((5,)),
            pltpu.SemaphoreType.DMA((24,)),
        ],
        compiler_params=pltpu.CompilerParams(vmem_limit_bytes=60 * 1024 * 1024),
    )(c.reshape(1).astype(jnp.int32), y.reshape(1).astype(jnp.int32), slot_sample, slot_sample.reshape(1, 160),
      prefix_keys.reshape(2560, width), prefix_values.reshape(2560, width), queries)
    met = lax.all_to_all(sent, ("prompt", "sample"), 0, 0, axis_index_groups=near, tiled=True)

    ids = jnp.arange(160, dtype=jnp.int32)
    wanted = y * slots + jnp.arange(slots, dtype=jnp.int32)
    slot_of = jnp.sum(jnp.where(slot_sample[None, :] == wanted[:, None], ids[None, :], 0), axis=1)
    at, from_row = slot_of % slots, slot_of // slots
    owner = slot_sample // slots
    ahead = (ids // slots == from_row[:, None]) & (ids < slot_of[:, None]) & (owner == y)
    rank = jnp.sum(ahead.astype(jnp.int32), axis=1)
    many = mode[0] > 0
    start = jnp.where(
        many,
        ((at // 20) * 4 + from_row) * 480 + (at % 20) * 8,
        ((rank % 2) * 4 + from_row) * 240 + (rank // 2) * 8,
    )

    def all_queries():
        half = lax.dynamic_slice_in_dim(queries, c * (slots // 2), slots // 2, 1)
        half = half.reshape(steps, slots // 2, key_heads, group, width)
        half = jnp.transpose(half, (2, 0, 1, 3, 4)).reshape(2, 1, 480, width)
        half = jnp.broadcast_to(half, (2, 4, 480, width)).reshape(8, 480, width)
        half = lax.all_to_all(half, ("prompt", "sample"), 0, 0, axis_index_groups=near, tiled=True)
        return half.reshape(3840, width)


    extra = lax.cond(many, all_queries, lambda: jnp.zeros((3840, width), BF16))

    odd = y % 2
    block = jnp.where(odd == 0, jnp.array([0, 0, 1, 1, 2], jnp.int32), jnp.array([0, 1, 1, 2, 2], jnp.int32))
    limit = jnp.take(prompt_lengths, (y * 5) // 2 + block) - z * 1024
    n = np.arange(192)
    order = np.zeros((192, 192), np.float32)
    order[n, ((n // 96) * 12 + n % 12) * 8 + (n % 96) // 12] = 1.0
    def rows(a):
        a = jnp.broadcast_to(a, (steps, slots) + a.shape[2:])
        a = a.reshape((steps, 2, 20) + a.shape[2:])
        a = jnp.swapaxes(a, 0, 1).reshape((2, 60) + a.shape[3:])
        return jnp.pad(a, [(0, 0), (0, 4)] + [(0, 0)] * (a.ndim - 2)).reshape((128,) + a.shape[2:])

    own_id = lax.dynamic_slice_in_dim(slot_sample, y * slots, slots, 0)
    from_y = (own_id // slots)[None, :]
    r = own_id % slots
    half = ((r % 8) // 4)[None, :]
    row = ((r // 8) * 12 + (r % 4) * 3)[None, :] + t_ids[:, None]
    going = jnp.take(unfinished, own_id // SAMPLES, axis=1)
    living = (own_id % SAMPLES)[None, :] < going
    place, lane = from_y * 64 + row, from_y * 128 + half * 64 + row

    qs = queries.reshape(steps, slots, key_heads, group, width)
    qs = lax.dynamic_slice(qs, (0, 0, c, z // 2, 0), (steps, slots, 1, 1, width))[:, :, 0, 0].astype(F32)

    def of_head(old, new, first, size):
        a = jnp.concatenate([old, jnp.swapaxes(new, 0, 1)], axis=1)
        return lax.dynamic_slice(a, (0, 0, c, first), a.shape[:2] + (1, size))[:, :, 0].astype(F32)

    keys = of_head(suffix_keys, new_keys, 0, width)
    values = of_head(suffix_values, new_values, (z % 2) * 64, 64)
    score = jnp.sum(qs[:, :, None] * keys[None], axis=-1) * scale
    u_ids = jnp.arange(keys.shape[1], dtype=jnp.int32)
    seen = (u_ids[None, :] <= suffix_keys.shape[1] + t_ids[:, None])[:, None, :]
    score = jnp.where(seen, score, MASKED)
    own_top = jnp.max(score, axis=2)
    weight = jnp.where(seen, jnp.exp(score - own_top[:, :, None]), 0.0)
    den = jnp.sum(weight, axis=2)
    num = jnp.sum(weight[..., None] * values[None], axis=2)
    own = jnp.stack([jnp.broadcast_to(a, (steps, slots)).astype(F32) for a in (place, lane, half, own_top, den, living)])
    own = jnp.swapaxes(own.reshape(6, steps, 2, 20), 1, 2).reshape(6, 2, 60)
    own = jnp.pad(own, ((0, 2), (0, 0), (0, 4))).reshape(8, 128)
    met, own, num, extra = lax.optimization_barrier((met, own, rows(num), extra))

    of_heads = np.zeros((8, 192), np.float32)
    of_heads[(n % 96) // 12, n] = 1.0
    part = pl.pallas_call(
        attend_kernel,
        in_specs=[SMEM, SMEM, SMEM, SMEM, VMEM, VMEM, VMEM, HBM],
        out_specs=VMEM,
        out_shape=jax.ShapeDtypeStruct((16, 64, 128), F32),
        scratch_shapes=[
            pltpu.VMEM((3840, 128), F32),
            pltpu.VMEM((5, 192, 128), F32),
            pltpu.VMEM((3840, 128), BF16),
            pltpu.SemaphoreType.DMA,
        ],
        compiler_params=PARAMS,
    )(many.astype(jnp.int32).reshape(1), block, limit, start, met, jnp.asarray(order, BF16), jnp.asarray(of_heads, F32), extra)

    got = lax.all_to_all(part.astype(jnp.float16), "prompt", 0, 0, axis_index_groups=same_core, tiled=True)

    part = pl.pallas_call(
        combine_kernel,
        in_specs=[VMEM],
        out_specs=VMEM,
        out_shape=jax.ShapeDtypeStruct((4, 64, 128), F32),
        compiler_params=PARAMS,
    )(got.astype(F32))
    every = lax.all_to_all(part, "sample", 0, 0, tiled=True)
    part = pl.pallas_call(
        finish_kernel,
        in_specs=[VMEM] * 3,
        out_specs=VMEM,
        out_shape=jax.ShapeDtypeStruct((16, 64, 128), BF16),
        compiler_params=PARAMS,
    )(every, own, num)

    mine = lax.all_to_all(part, "prompt", 0, 0, axis_index_groups=same_core, tiled=True)
    other = lax.ppermute(mine, "prompt", [(i, i ^ 1) for i in range(32)])
    mine = pl.pallas_call(
        own_lay_kernel,
        in_specs=[VMEM],
        out_specs=VMEM,
        out_shape=jax.ShapeDtypeStruct((120, 8, 128), F32),
        compiler_params=PARAMS,
        cost_estimate=pl.CostEstimate(flops=1000000, bytes_accessed=1500000, transcendentals=0),
    )(mine)
    return pl.pallas_call(
        final_kernel,
        in_specs=[SMEM, VMEM, VMEM],
        out_specs=VMEM,
        out_shape=jax.ShapeDtypeStruct((steps, slots, heads, width), BF16),
        scratch_shapes=[pltpu.VMEM((120, 16, 128), F32)],
        compiler_params=PARAMS,
    )(c.reshape(1).astype(jnp.int32), mine, other)


def solution(mesh):
    in_specs = (
        P(None, "sample", "tensor", None),
        P(None, ("prompt", "sample"), "tensor", None),
        P(None, ("prompt", "sample"), "tensor", None),
        P("sample", None, "tensor", None),
        P("sample", None, "tensor", None),
        P(None, "sample", "tensor", None),
        P(None, "sample", "tensor", None),
        P(),
        P(),
        P(),
    )
    out_specs = P(None, "sample", "tensor", None)
    return jax.shard_map(shards, mesh=mesh, in_specs=in_specs, out_specs=out_specs, check_vma=False)
```
